256 devices in a mesh: role: 2 (over core), grp: 8 (over z), dp: 16 (over y, x).
Axes of the slice: x: 4, y: 4, z: 8, core: 2. Of those that a mesh axis runs over, the one named last changes fastest.
Arguments:
- attn_parts: bfloat16 [8, 1536, 7168], P('grp', 'role', 'dp'), may hold values from -3 to 3
- residual: bfloat16 [1536, 7168], P(('role', 'grp', 'dp')), may hold values from -6 to 6
- norm_gain: bfloat16 [7168], replicated, may hold values from 0.099609375 to 1.8984375
- router_weight: bfloat16 [7168, 32], replicated, may hold values from -0.0625 to 0.0625
- expert_ids: int32 [1536, 8], P(('role', 'grp', 'dp')), may hold values from 0 to 31, all different within a row; in each aligned block of 6 rows (0 to 5, 6 to 11, ...) at most 2 rows name the same one
- w_gate: bfloat16 [32, 7168, 2048], P(('role', 'dp'), None, 'grp'), may hold values from -0.0625 to 0.0625
- w_up: bfloat16 [32, 7168, 2048], P(('role', 'dp'), None, 'grp'), may hold values from -0.0625 to 0.0625
- w_down: bfloat16 [32, 2048, 7168], P(('role', 'dp'), 'grp'), may hold values from -0.125 to 0.125
Outputs:
- mixed: bfloat16 [1536, 7168], P(('role', 'grp', 'dp'))
The draws below stay inside these ranges and needn't reach their ends.
Inputs may be any that keep to these rules, and one draw needn't show every extreme that they name: `expert_ids`: each row names 8 different experts. Among the 6 rows of one device no expert is named by more than 2 rows, and in every draw the rows of some device name some expert exactly 2 times.
All inputs are finite; a program needn't handle non-finite values.
Results may differ from the reference program's by a relative error of at most 0.012.
Values may be sent and summed in bfloat16 or wider, within the bound.
No kernel may reach another device: no remote copies, remote signals or barrier semaphores. Data moves between devices by JAX's collectives and lax.ppermute only.
A program may use at most 128 MiB of HBM per device.

```python
import math
import jax
import jax.numpy as jnp
import numpy as np
from jax import lax

D = 7168
FF = 2048
TOP = 8
EXPERTS = 32
ROW_DEV = 6
CAP = 2
HEAD_GROUPS = 8
ROWS = 1536
N_GRP = 8


def shard_levels(rng, shape, split, least, top_value):
    gain, own = 1.0, jax.random.fold_in(rng, 6)
    for dim, shards_of in split:
        heights = jnp.exp(jax.random.uniform(jax.random.fold_in(own, dim), (shards_of,), jnp.float32, least / len(split), top_value / len(split)))
        gain = gain * jnp.repeat(heights, shape[dim] // shards_of).reshape([-1 if axis == dim else 1 for axis in range(len(shape))])
    return gain


def assign_block(own_key, own, number, rows, amount, top, reach, lean):
    sequence = jax.random.permutation(own_key, amount)
    heavy_load, usual = portions_of(amount, rows * top, reach, lean, True), portions_of(amount, rows * top, reach, lean, False)
    places = jnp.arange(amount)

    def named(lengths, offset_by):
        used = int((lengths > 0).sum())
        fixed = max(1, used // 4)
        shifted = fixed + (places - fixed + offset_by * (used - fixed)) % max(1, amount - fixed)
        return jnp.zeros((amount,), jnp.int32).at[sequence[jnp.where(places < fixed, places, shifted)]].set(jnp.asarray(lengths, jnp.int32))

    lengths = jnp.where(number % 4 == 0, named(heavy_load, number // 4), named(usual, number - number // 4 - 1))
    mixed = jax.random.permutation(jax.random.fold_in(own, 3), amount)
    giver, taker = mixed[0:amount // 2 * 2:2], mixed[1:amount // 2 * 2:2]
    slack = jnp.minimum(lengths[giver] - 1, reach - lengths[taker]) // 2
    slack = jnp.where((giver == sequence[0]) | (taker == sequence[0]) | (lengths[taker] == 0), 0, jnp.maximum(slack, 0))
    shifted = jax.random.randint(jax.random.fold_in(own, 4), (amount // 2,), 0, 1 << 20) % (slack + 1)
    lengths = lengths.at[giver].add(-shifted).at[taker].add(shifted)
    items = jnp.searchsorted(jnp.cumsum(lengths), jnp.arange(rows * top), side="right").astype(jnp.int32)
    table = items.reshape(top, rows).T
    table = table[jax.random.permutation(jax.random.fold_in(own, 1), rows)]
    offset_by = jax.random.randint(jax.random.fold_in(own, 2), (rows, 1), 0, top)
    return jnp.take_along_axis(table, (jnp.arange(top)[None, :] + offset_by) % top, axis=1)


def portions_of(number_of, total, most, lean, full):
    loads = [(1 << 20) // math.isqrt(standing ** lean) + 1 for standing in range(1, number_of + 1)]
    largest = most if full else min(most, max(-(-total // number_of), total * loads[0] // sum(loads)))
    least = 1 if total - largest >= number_of - 1 else 0
    holding, rest = [largest] + [least] * (number_of - 1), total - largest - least * (number_of - 1)
    while rest > 0:
        free = [i for i in range(1, number_of) if holding[i] < largest] or [i for i in range(1, number_of) if holding[i] < most]
        mass, left = sum([loads[i] for i in free]), rest
        for i in free:
            extra = min(most - holding[i], max(1, left * loads[i] // mass), rest)
            holding[i] = holding[i] + extra
            rest = rest - extra
    return np.array(holding)


def gaussian(own_key, dims, deviation, bound, cuts=(), kind=jnp.bfloat16):
    values = jax.random.normal(own_key, dims, jnp.float32) * deviation
    if len(cuts) > 0:
        values = shard_levels(own_key, dims, cuts, -0.22, 0.18) * values
    return jnp.clip(values, min=-bound, max=bound).astype(kind)


def setup_inputs(seed: int = 0) -> dict:
    splits = jax.random.split(jax.random.key(seed), 9)
    attn_parts = gaussian(splits[0], (HEAD_GROUPS, ROWS, D), 0.5, 3.0, ((0, 8), (1, 2), (2, 16)))
    residual = gaussian(splits[1], (ROWS, D), 1.0, 6.0, ((0, 256),))
    norm_gain = jnp.clip(1.0 + 0.18 * jax.random.normal(splits[2], (D,), jnp.float32), 0.099609375, 1.8984375).astype(jnp.bfloat16)
    router_weight = gaussian(splits[3], (D, EXPERTS), D ** -0.5, 0.0625)
    expert_ids_keys = jax.random.split(jax.random.fold_in(splits[4], 1), ROWS // ROW_DEV)
    expert_ids_turns = jax.random.permutation(jax.random.fold_in(splits[4], 3), ROWS // ROW_DEV)
    expert_ids = jax.vmap(lambda own, number: assign_block(jax.random.fold_in(splits[4], 2), own, number, ROW_DEV, EXPERTS, TOP, CAP, 2))(expert_ids_keys, expert_ids_turns).reshape((ROWS, TOP))
    w_gate = gaussian(splits[5], (EXPERTS, D, FF), D ** -0.5, 0.0625, ((0, 32), (2, 8)))
    w_up = gaussian(splits[6], (EXPERTS, D, FF), D ** -0.5, 0.0625, ((0, 32), (2, 8)))
    w_down = gaussian(splits[7], (EXPERTS, FF, D), FF ** -0.5, 0.125, ((0, 32), (1, 8)))
    return {"attn_parts": attn_parts, "residual": residual, "norm_gain": norm_gain, "router_weight": router_weight, "expert_ids": expert_ids, "w_gate": w_gate, "w_up": w_up, "w_down": w_down}


norm_eps = 1e-06
route_scale = 2.5

def slot_table(expert_ids):
    blocks = expert_ids.shape[0] // ROW_DEV
    block_ids = expert_ids.reshape(blocks, ROW_DEV, TOP)
    onehot = (block_ids[..., None] == jnp.arange(EXPERTS, dtype=jnp.int32)).astype(jnp.float32)
    chosen = lax.optimization_barrier(jnp.sum(onehot, axis=2))
    slot_rank = jnp.cumsum(chosen, axis=1) - chosen
    slot_index = jnp.arange(CAP, dtype=jnp.int32).astype(jnp.float32)
    select = chosen[..., None] * (slot_rank[..., None] == slot_index).astype(jnp.float32)
    return (onehot, select)

def reference(attn_parts, residual, norm_gain, router_weight, expert_ids, w_gate, w_up, w_down):
    attention = lax.optimization_barrier(jnp.sum(attn_parts.astype(jnp.float32), axis=0))
    hidden = (residual.astype(jnp.float32) + attention).astype(jnp.bfloat16)
    hidden_f = hidden.astype(jnp.float32)
    meansq = lax.optimization_barrier(jnp.mean(hidden_f * hidden_f, axis=-1, keepdims=True))
    normed = (hidden_f * lax.rsqrt(meansq + norm_eps) * norm_gain.astype(jnp.float32)).astype(jnp.bfloat16)
    scores = jax.nn.sigmoid(jnp.dot(normed, router_weight, preferred_element_type=jnp.float32))
    onehot, select = slot_table(expert_ids)
    blocks = select.shape[0]
    picked = lax.optimization_barrier(jnp.sum(onehot * scores.reshape(blocks, ROW_DEV, 1, EXPERTS), axis=-1))
    weights = route_scale * picked / lax.optimization_barrier(jnp.sum(picked, axis=-1, keepdims=True))
    per_expert = lax.optimization_barrier(jnp.sum(onehot * weights[..., None], axis=2))
    rows_block = normed.reshape(blocks, ROW_DEV, D).astype(jnp.float32)
    shard_width = FF // N_GRP

    def expert_step(totals, expert):
        chosen_slots = select[:, :, expert, :]
        inputs = jnp.einsum('brc,brd->bcd', chosen_slots, rows_block).astype(jnp.bfloat16).reshape(blocks * CAP, D)
        gate_val = jnp.dot(inputs, w_gate[expert], preferred_element_type=jnp.float32)
        up_val = jnp.dot(inputs, w_up[expert], preferred_element_type=jnp.float32)
        gated = (jax.nn.silu(gate_val) * up_val).astype(jnp.bfloat16)
        partials = jnp.einsum('spf,pfd->spd', gated.reshape(blocks * CAP, N_GRP, shard_width).astype(jnp.float32), w_down[expert].reshape(N_GRP, shard_width, D).astype(jnp.float32))
        partials = lax.optimization_barrier(partials.astype(jnp.bfloat16))
        expert_out = lax.optimization_barrier(jnp.sum(partials.astype(jnp.float32), axis=1)).astype(jnp.bfloat16)
        outputs = expert_out.reshape(blocks, CAP, D).astype(jnp.float32)
        combine_mat = chosen_slots * per_expert[:, :, expert][..., None]
        return (totals + jnp.einsum('brc,bcd->brd', combine_mat, outputs), None)
    totals, _ = lax.scan(expert_step, jnp.zeros((blocks, ROW_DEV, D), jnp.float32), jnp.arange(EXPERTS, dtype=jnp.int32))
    routed = totals.reshape(blocks * ROW_DEV, D)
    return (hidden_f + routed).astype(jnp.bfloat16)
```

```python
import functools

import jax
import jax.numpy as jnp
from jax import lax
from jax.experimental import pallas as pl
from jax.experimental.pallas import tpu as pltpu
from jax.sharding import PartitionSpec as P

CAP = 2
B_COLS = 2560
UP_CHUNK = 1024
DOWN_CHUNK = 1024
VMEM_MIB = 40
AUX = 128
NO_EXPERT = 99.0

norm_eps = 1e-06
route_scale = 2.5
f32 = jnp.float32
bf16 = jnp.bfloat16


def iota(shape, dim):
    return lax.broadcasted_iota(jnp.int32, shape, dim)


def dot(a, b, contract=((1,), (0,))):
    return lax.dot_general(a, b, (contract, ((), ())), preferred_element_type=f32)


def split3(x):
    hi = x.astype(bf16)
    rest = x - hi.astype(f32)
    mid = rest.astype(bf16)
    lo = (rest - mid.astype(f32)).astype(bf16)
    return hi, mid, lo


def params():
    return pltpu.CompilerParams(vmem_limit_bytes=VMEM_MIB * 1024 * 1024)


def slots_of(ids, weight_cols, rows, rows_block, experts, per_expert_cols):
    blocks = rows // rows_block
    lane = iota((rows, experts), 1).astype(f32)
    chosen = jnp.zeros((rows, experts), f32)
    per_expert = jnp.zeros((rows, experts), f32)
    for k in range(len(weight_cols)):
        match = (ids[:, k : k + 1] == lane).astype(f32)
        chosen = chosen + match
        per_expert = per_expert + match * weight_cols[k]
    r, c = iota((rows, rows), 0), iota((rows, rows), 1)
    before = ((r // rows_block == c // rows_block) & (c < r)).astype(f32).astype(bf16)
    rank = dot(before, chosen.astype(bf16))
    cols = experts * per_expert_cols
    spread = (iota((experts, cols), 1) // per_expert_cols == iota((experts, cols), 0)).astype(f32).astype(bf16)
    hi, mid, lo = split3(per_expert)
    chosen_x = dot(chosen.astype(bf16), spread)
    rank_x = dot(rank.astype(bf16), spread)
    weight_x = dot(hi, spread) + dot(mid, spread) + dot(lo, spread)
    col = iota((rows, cols), 1)
    own = (col // CAP) % blocks == iota((rows, cols), 0) // rows_block
    select = jnp.where(own & (rank_x == (col % CAP).astype(f32)), chosen_x, 0.0)
    return select, select * weight_x


def route_body(rows_dev, top, experts, ca, hidden_ref, gain_ref, router_ref, ids_ref, out_ref, payload_ref, comb_ref):
    h = hidden_ref[...].astype(f32)
    rows, width = h.shape
    meansq = jnp.sum(h * h, axis=-1, keepdims=True) * (1.0 / width)
    normed = (h * lax.rsqrt(meansq + norm_eps) * gain_ref[...].astype(f32)).astype(bf16)
    scores = jax.nn.sigmoid(dot(normed, router_ref[...], ((1,), (1,))))
    ids = ids_ref[...].astype(f32)
    lane = iota((rows, experts), 1).astype(f32)
    picked = [
        jnp.sum(jnp.where(ids[:, k : k + 1] == lane, scores, 0.0), axis=-1, keepdims=True) for k in range(top)
    ]
    total = functools.reduce(lambda a, b: a + b, picked)
    total = jnp.where(iota((rows, 1), 0) < rows_dev, total, 1.0)
    weights = [route_scale * p / total for p in picked]
    select, combine = slots_of(ids, weights, rows, rows, experts, CAP)
    hi, mid, _ = split3(combine)
    comb_ref[:rows, :] = hi.astype(f32)
    comb_ref[rows:, :] = mid.astype(f32)
    out_ref[...] = dot(select.astype(bf16), normed[:, :ca], ((0,), (0,))).astype(bf16)
    payload_ref[:, : width - ca] = normed[:, ca:]
    at = iota((rows, AUX), 1)
    aux = jnp.zeros((rows, AUX), f32)
    for k in range(top):
        aux = jnp.where(at == k, ids[:, k : k + 1], aux)
        for part, value in enumerate(split3(weights[k])):
            aux = jnp.where(at == (part + 1) * top + k, value.astype(f32), aux)
    payload_ref[:, width - ca :] = aux.astype(bf16)


def route(hidden, gain, router_t, ids, rows_dev, ca):
    rows, width = hidden.shape
    experts, top = router_t.shape[0], ids.shape[1]
    return pl.pallas_call(
        functools.partial(route_body, rows_dev, top, experts, ca),
        out_shape=(
            jax.ShapeDtypeStruct((experts * CAP, ca), bf16),
            jax.ShapeDtypeStruct((rows, width - ca + AUX), bf16),
            jax.ShapeDtypeStruct((2 * rows, experts * CAP), f32),
        ),
        compiler_params=params(),
        name="route",
    )(hidden, gain, router_t, ids)


def spread_body(top, experts, rows_block, rows_ref, out_ref, comb_ref):
    rows = rows_ref.shape[0]
    blocks = rows // rows_block
    cb = rows_ref.shape[1] - AUX
    aux = rows_ref[:, cb:].astype(f32)
    ids = aux[:, :top]
    weights = [
        aux[:, top + k : top + k + 1] + aux[:, 2 * top + k : 2 * top + k + 1] + aux[:, 3 * top + k : 3 * top + k + 1]
        for k in range(top)
    ]
    select, combine = slots_of(ids, weights, rows, rows_block, experts, blocks * CAP)
    hi, mid, _ = split3(combine)
    comb_ref[:rows, :] = hi
    comb_ref[rows:, :] = mid
    out_ref[...] = dot(select.astype(bf16), rows_ref[:, :cb], ((0,), (0,))).astype(bf16)


def spread_rows(rows_in, top, experts, rows_block):
    rows, width = rows_in.shape
    slots = experts * (rows // rows_block) * CAP
    return pl.pallas_call(
        functools.partial(spread_body, top, experts, rows_block),
        out_shape=(
            jax.ShapeDtypeStruct((slots, width - AUX), bf16),
            jax.ShapeDtypeStruct((2 * rows, slots), bf16),
        ),
        compiler_params=params(),
        name="spread_rows",
    )(rows_in)


def reorder(slots, blocks, groups, to_block_major):
    row, col = iota((slots, slots), 0), iota((slots, slots), 1)
    if to_block_major:
        outer, inner = groups, blocks
    else:
        outer, inner = blocks, groups
    first, second, slot = row // (outer * CAP), (row // CAP) % outer, row % CAP
    return (col == (second * inner + first) * CAP + slot).astype(f32).astype(bf16)


def chunks_of(start, stop, size):
    return [(at, min(size, stop - at)) for at in range(start, stop, size)]


def loads(pieces, sem):
    copies = [pltpu.make_async_copy(src, dst, sem.at[i]) for i, (src, dst) in enumerate(pieces)]
    for copy in copies:
        copy.start()
    return copies


def up_loads(pieces, base, x_hbm, wg_hbm, wu_hbm, x_buf, wg_buf, wu_buf):
    out = []
    for at, size in pieces:
        here, there = pl.ds(at - base, size), pl.ds(at, size)
        out.append((x_hbm.at[:, here], x_buf.at[:, here]))
        out.append((wg_hbm.at[0, there, :], wg_buf.at[here, :]))
        out.append((wu_hbm.at[0, there, :], wu_buf.at[here, :]))
    return out


def up_sums(pieces, base, copies, x_buf, wg_buf, wu_buf, acc):
    ff = wg_buf.shape[1]
    for i, (at, size) in enumerate(pieces):
        for copy in copies[3 * i : 3 * i + 3]:
            copy.wait()
        here = pl.ds(at - base, size)
        x = x_buf[:, here]
        gate, up = dot(x, wg_buf[here, :]), dot(x, wu_buf[here, :])
        if i == 0:
            acc[:, :ff] = gate
            acc[:, ff:] = up
        else:
            acc[:, :ff] += gate
            acc[:, ff:] += up


def up_first_body(blocks, groups, base, x_hbm, wg_hbm, wu_hbm, part_ref, x_buf, wg_buf, wu_buf, acc, sem):
    pieces = chunks_of(base, wg_hbm.shape[1], UP_CHUNK)
    copies = loads(up_loads(pieces, base, x_hbm, wg_hbm, wu_hbm, x_buf, wg_buf, wu_buf), sem)
    order = reorder(acc.shape[0], blocks, groups, True)
    up_sums(pieces, base, copies, x_buf, wg_buf, wu_buf, acc)
    hi, mid, lo = split3(acc[...])
    part_ref[...] = dot(order, hi) + dot(order, mid) + dot(order, lo)


def up_first(x, w_gate, w_up, blocks, groups):
    slots, width = x.shape
    _, total, ff = w_gate.shape
    copies = 3 * len(chunks_of(total - width, total, UP_CHUNK))
    return pl.pallas_call(
        functools.partial(up_first_body, blocks, groups, total - width),
        in_specs=[pl.BlockSpec(memory_space=pl.ANY)] + [pl.BlockSpec(memory_space=pltpu.HBM)] * 2,
        out_shape=jax.ShapeDtypeStruct((slots, 2 * ff), f32),
        scratch_shapes=[
            pltpu.VMEM((slots, width), bf16),
            pltpu.VMEM((width, ff), bf16),
            pltpu.VMEM((width, ff), bf16),
            pltpu.VMEM((slots, 2 * ff), f32),
            pltpu.SemaphoreType.DMA((copies,)),
        ],
        compiler_params=params(),
        cost_estimate=pl.CostEstimate(
            flops=4 * slots * width * ff, bytes_accessed=2 * width * (slots + 2 * ff), transcendentals=0
        ),
        name="up_first",
    )(x, w_gate, w_up)


def rest_body(blocks, groups, part_hbm, x_hbm, wg_hbm, wu_hbm, wd_hbm, y_hbm, act_ref, *scratch):
    part_buf, x_buf, wg_buf, wu_buf, wd_buf, y_buf, acc, sem, y_sem = scratch
    slots, width = x_hbm.shape
    ff = wg_hbm.shape[2]
    pieces = chunks_of(0, width, UP_CHUNK)
    downs = chunks_of(0, width, DOWN_CHUNK)
    wanted = up_loads(pieces, 0, x_hbm, wg_hbm, wu_hbm, x_buf, wg_buf, wu_buf)
    wanted.append((part_hbm, part_buf))
    wanted.append((wd_hbm.at[0, :, pl.ds(0, width)], wd_buf))
    copies = loads(wanted, sem)
    up_sums(pieces, 0, copies, x_buf, wg_buf, wu_buf, acc)
    copies[-2].wait()
    gate = acc[:, :ff] + part_buf[:, :ff]
    up = acc[:, ff:] + part_buf[:, ff:]
    act = (gate / (1.0 + jnp.exp(-gate)) * up).astype(bf16)
    act_ref[...] = act
    copies[-1].wait()
    out = []
    for i, (at, size) in enumerate(downs):
        here = pl.ds(at, size)
        y_buf[:, here] = dot(act_ref[...], wd_buf[:, here]).astype(bf16)
        copy = pltpu.make_async_copy(y_buf.at[:, here], y_hbm.at[:, here], y_sem.at[i])
        copy.start()
        out.append(copy)
    for copy in out:
        copy.wait()


def up_rest_down(part, x, w_gate, w_up, w_down, blocks, groups):
    slots, width = x.shape
    ff = w_gate.shape[2]
    copies = 3 * len(chunks_of(0, width, UP_CHUNK)) + 2
    return pl.pallas_call(
        functools.partial(rest_body, blocks, groups),
        in_specs=[pl.BlockSpec(memory_space=pl.ANY)] + [pl.BlockSpec(memory_space=pltpu.HBM)] * 4,
        out_specs=[pl.BlockSpec(memory_space=pltpu.HBM), pl.BlockSpec(memory_space=pltpu.VMEM)],
        out_shape=(pltpu.HBM((slots, width), bf16), jax.ShapeDtypeStruct((slots, ff), bf16)),
        scratch_shapes=[
            pltpu.VMEM((slots, 2 * ff), f32),
            pltpu.VMEM((slots, width), bf16),
            pltpu.VMEM((width, ff), bf16),
            pltpu.VMEM((width, ff), bf16),
            pltpu.VMEM((ff, width), bf16),
            pltpu.VMEM((slots, width), bf16),
            pltpu.VMEM((slots, 2 * ff), f32),
            pltpu.SemaphoreType.DMA((copies,)),
            pltpu.SemaphoreType.DMA((len(chunks_of(0, width, DOWN_CHUNK)),)),
        ],
        compiler_params=params(),
        cost_estimate=pl.CostEstimate(
            flops=6 * slots * width * ff, bytes_accessed=2 * width * (2 * slots + 3 * ff), transcendentals=slots * ff
        ),
        name="up_rest_down",
    )(part, x, w_gate, w_up, w_down)


def down_body(blocks, groups, act_ref, wd_hbm, out_ref, wd_buf, act_buf, sem):
    slots, width = out_ref.shape
    base = wd_hbm.shape[2] - width
    downs = chunks_of(0, width, DOWN_CHUNK)
    copies = loads([(wd_hbm.at[0, :, pl.ds(base + at, size)], wd_buf.at[:, pl.ds(at, size)]) for at, size in downs], sem)
    act_buf[...] = dot(reorder(slots, blocks, groups, False), act_ref[...]).astype(bf16)
    for copy, (at, size) in zip(copies, downs):
        copy.wait()
        out_ref[:, pl.ds(at, size)] = dot(act_buf[...], wd_buf[:, pl.ds(at, size)]).astype(bf16)


def down(act, w_down, width, blocks, groups):
    slots, ff = act.shape
    return pl.pallas_call(
        functools.partial(down_body, blocks, groups),
        in_specs=[pl.BlockSpec(memory_space=pltpu.VMEM), pl.BlockSpec(memory_space=pltpu.HBM)],
        out_shape=jax.ShapeDtypeStruct((slots, width), bf16),
        scratch_shapes=[
            pltpu.VMEM((ff, width), bf16),
            pltpu.VMEM((slots, ff), bf16),
            pltpu.SemaphoreType.DMA((len(chunks_of(0, width, DOWN_CHUNK)),)),
        ],
        compiler_params=params(),
        cost_estimate=pl.CostEstimate(
            flops=2 * slots * width * ff, bytes_accessed=2 * width * (slots + ff), transcendentals=0
        ),
        name="down",
    )(act, w_down)


def local(attn_parts, residual, norm_gain, router_weight, expert_ids, w_gate, w_up, w_down):
    blocks = lax.axis_size("grp")
    dp_count = lax.axis_size("dp")
    groups = lax.axis_size("role") * dp_count
    plane = ("role", "dp")
    rows_dev, width = residual.shape
    experts = router_weight.shape[1]
    top = expert_ids.shape[1]
    cb = B_COLS
    ca = width - cb
    rows_pad = 8

    part = attn_parts[0]
    col_width = part.shape[1]
    tiles = -(-col_width // 128)
    pieces = jnp.pad(part, ((0, 0), (0, tiles * 128 - col_width)))
    pieces = pieces.reshape(blocks * dp_count, rows_dev * tiles, 128)
    received = lax.all_to_all(pieces, ("grp", "dp"), split_axis=0, concat_axis=0, tiled=True)
    received = received.reshape(blocks, dp_count, rows_dev * tiles, 128)
    attention = jnp.sum(received.astype(f32), axis=0)
    attention = attention.reshape(dp_count, rows_dev, tiles * 128)[:, :, :col_width]
    attention = attention.transpose(1, 0, 2).reshape(rows_dev, width)
    hidden = (residual.astype(f32) + attention).astype(bf16)
    hidden = jnp.pad(hidden, ((0, rows_pad - rows_dev), (0, 0)))

    ids = jnp.pad(expert_ids, ((0, rows_pad - rows_dev), (0, 0)), constant_values=int(NO_EXPERT))
    out_a, payload, comb_a = route(hidden, norm_gain[None], router_weight.T, ids, rows_dev, ca)

    arrived = lax.all_to_all(out_a.reshape(groups, CAP, ca), plane, split_axis=0, concat_axis=0, tiled=True)
    arrived = arrived.reshape(groups * CAP, ca)
    arrived, payload = lax.optimization_barrier((arrived, payload))
    x_a = lax.all_gather(arrived, "grp", axis=0, tiled=True)

    copies = jnp.broadcast_to(payload[None], (blocks, rows_pad, cb + AUX))
    column = lax.all_to_all(copies, "grp", split_axis=0, concat_axis=0, tiled=True)
    out_b, comb_b = spread_rows(column.reshape(blocks * rows_pad, cb + AUX), top, experts, rows_pad)
    x_b = lax.all_to_all(out_b.reshape(groups, blocks * CAP, cb), plane, split_axis=0, concat_axis=0, tiled=True)
    x_b = x_b.reshape(groups * blocks * CAP, cb)

    w_gate, w_up, w_down, x_a = (
        pltpu.with_memory_space_constraint(w, pltpu.HBM) for w in (w_gate, w_up, w_down, x_a)
    )
    part_up = up_first(x_b, w_gate, w_up, blocks, groups)
    y_a, act = up_rest_down(part_up, x_a, w_gate, w_up, w_down, blocks, groups)
    sum_a = lax.psum_scatter(y_a, "grp", scatter_dimension=0, tiled=True)

    y_b = down(act, w_down, cb, blocks, groups)
    back_b = lax.all_to_all(y_b.reshape(groups, blocks * CAP, cb), plane, split_axis=0, concat_axis=0, tiled=True)
    mixed_b = dot(comb_b, back_b.reshape(groups * blocks * CAP, cb))
    mixed_b = (mixed_b[: blocks * rows_pad] + mixed_b[blocks * rows_pad :]).astype(bf16)
    mixed_b = mixed_b.reshape(blocks, rows_pad, cb)
    mixed_b = lax.all_to_all(mixed_b, "grp", split_axis=0, concat_axis=0, tiled=True)
    routed_b = jnp.sum(mixed_b.astype(f32), axis=0)[:rows_dev]

    sum_a, routed_b = lax.optimization_barrier((sum_a, routed_b))
    back_a = lax.all_to_all(sum_a.reshape(groups, CAP, ca), plane, split_axis=0, concat_axis=0, tiled=True)
    routed_a = dot(comb_a.astype(bf16), back_a.reshape(groups * CAP, ca))
    routed_a = routed_a[:rows_dev] + routed_a[rows_pad : rows_pad + rows_dev]
    routed = jnp.concatenate([routed_a, routed_b], axis=1)
    return (hidden[:rows_dev].astype(f32) + routed).astype(bf16)


def solution(mesh):
    in_specs = (
        P("grp", "role", "dp"),
        P(("role", "grp", "dp"), None),
        P(),
        P(),
        P(("role", "grp", "dp"), None),
        P(("role", "dp"), None, "grp"),
        P(("role", "dp"), None, "grp"),
        P(("role", "dp"), "grp", None),
    )
    out_specs = P(("role", "grp", "dp"), None)
    return jax.shard_map(local, mesh=mesh, in_specs=in_specs, out_specs=out_specs, check_vma=False)
```

```python
import functools

import jax
import jax.numpy as jnp
from jax import lax
from jax.experimental import pallas as pl
from jax.experimental.pallas import tpu as pltpu
from jax.sharding import PartitionSpec as P

CAP = 2
B_OUT = 2560
B_BACK = 2688
UP_CHUNK = 1024
DOWN_CHUNK = 1024
VMEM_MIB = 40
AUX = 128
NO_EXPERT = 99.0

norm_eps = 1e-06
route_scale = 2.5
f32 = jnp.float32
bf16 = jnp.bfloat16


def iota(shape, dim):
    return lax.broadcasted_iota(jnp.int32, shape, dim)


def dot(a, b, contract=((1,), (0,))):
    return lax.dot_general(a, b, (contract, ((), ())), preferred_element_type=f32)


def split3(x):
    hi = x.astype(bf16)
    rest = x - hi.astype(f32)
    mid = rest.astype(bf16)
    lo = (rest - mid.astype(f32)).astype(bf16)
    return hi, mid, lo


def params():
    return pltpu.CompilerParams(vmem_limit_bytes=VMEM_MIB * 1024 * 1024)


def slots_of(ids, weight_cols, rows, rows_block, experts, per_expert_cols):
    blocks = rows // rows_block
    lane = iota((rows, experts), 1).astype(f32)
    chosen = jnp.zeros((rows, experts), f32)
    per_expert = jnp.zeros((rows, experts), f32)
    for k in range(len(weight_cols)):
        match = (ids[:, k : k + 1] == lane).astype(f32)
        chosen = chosen + match
        per_expert = per_expert + match * weight_cols[k]
    r, c = iota((rows, rows), 0), iota((rows, rows), 1)
    before = ((r // rows_block == c // rows_block) & (c < r)).astype(f32).astype(bf16)
    rank = dot(before, chosen.astype(bf16))
    cols = experts * per_expert_cols
    spread = (iota((experts, cols), 1) // per_expert_cols == iota((experts, cols), 0)).astype(f32).astype(bf16)
    hi, mid, lo = split3(per_expert)
    chosen_x = dot(chosen.astype(bf16), spread)
    rank_x = dot(rank.astype(bf16), spread)
    weight_x = dot(hi, spread) + dot(mid, spread) + dot(lo, spread)
    col = iota((rows, cols), 1)
    own = (col // CAP) % blocks == iota((rows, cols), 0) // rows_block
    select = jnp.where(own & (rank_x == (col % CAP).astype(f32)), chosen_x, 0.0)
    return select, select * weight_x


def route_body(rows_dev, top, experts, ca, hidden_ref, gain_ref, router_ref, ids_ref, out_ref, payload_ref, comb_ref):
    h = hidden_ref[...].astype(f32)
    rows, width = h.shape
    meansq = jnp.sum(h * h, axis=-1, keepdims=True) * (1.0 / width)
    normed = (h * lax.rsqrt(meansq + norm_eps) * gain_ref[...].astype(f32)).astype(bf16)
    scores = jax.nn.sigmoid(dot(normed, router_ref[...], ((1,), (1,))))
    ids = ids_ref[...].astype(f32)
    lane = iota((rows, experts), 1).astype(f32)
    picked = [
        jnp.sum(jnp.where(ids[:, k : k + 1] == lane, scores, 0.0), axis=-1, keepdims=True) for k in range(top)
    ]
    total = functools.reduce(lambda a, b: a + b, picked)
    total = jnp.where(iota((rows, 1), 0) < rows_dev, total, 1.0)
    weights = [route_scale * p / total for p in picked]
    select, combine = slots_of(ids, weights, rows, rows, experts, CAP)
    hi, mid, _ = split3(combine)
    comb_ref[:rows, :] = hi.astype(f32)
    comb_ref[rows:, :] = mid.astype(f32)
    out_ref[...] = dot(select.astype(bf16), normed[:, :ca], ((0,), (0,))).astype(bf16)
    payload_ref[:, : width - ca] = normed[:, ca:]
    at = iota((rows, AUX), 1)
    aux = jnp.zeros((rows, AUX), f32)
    for k in range(top):
        aux = jnp.where(at == k, ids[:, k : k + 1], aux)
        for part, value in enumerate(split3(weights[k])):
            aux = jnp.where(at == (part + 1) * top + k, value.astype(f32), aux)
    payload_ref[:, width - ca :] = aux.astype(bf16)


def route(hidden, gain, router_t, ids, rows_dev, ca):
    rows, width = hidden.shape
    experts, top = router_t.shape[0], ids.shape[1]
    return pl.pallas_call(
        functools.partial(route_body, rows_dev, top, experts, ca),
        out_shape=(
            jax.ShapeDtypeStruct((experts * CAP, ca), bf16),
            jax.ShapeDtypeStruct((rows, width - ca + AUX), bf16),
            jax.ShapeDtypeStruct((2 * rows, experts * CAP), f32),
        ),
        compiler_params=params(),
        name="route",
    )(hidden, gain, router_t, ids)


def spread_body(top, experts, rows_block, rows_ref, out_ref, comb_ref):
    rows = rows_ref.shape[0]
    blocks = rows // rows_block
    cb = rows_ref.shape[1] - AUX
    aux = rows_ref[:, cb:].astype(f32)
    ids = aux[:, :top]
    weights = [
        aux[:, top + k : top + k + 1] + aux[:, 2 * top + k : 2 * top + k + 1] + aux[:, 3 * top + k : 3 * top + k + 1]
        for k in range(top)
    ]
    select, combine = slots_of(ids, weights, rows, rows_block, experts, blocks * CAP)
    hi, mid, _ = split3(combine)
    comb_ref[:rows, :] = hi
    comb_ref[rows:, :] = mid
    out_ref[...] = dot(select.astype(bf16), rows_ref[:, :cb], ((0,), (0,))).astype(bf16)


def spread_rows(rows_in, top, experts, rows_block):
    rows, width = rows_in.shape
    slots = experts * (rows // rows_block) * CAP
    return pl.pallas_call(
        functools.partial(spread_body, top, experts, rows_block),
        out_shape=(
            jax.ShapeDtypeStruct((slots, width - AUX), bf16),
            jax.ShapeDtypeStruct((2 * rows, slots), bf16),
        ),
        compiler_params=params(),
        name="spread_rows",
    )(rows_in)


def reorder(slots, blocks, groups, to_block_major):
    row, col = iota((slots, slots), 0), iota((slots, slots), 1)
    if to_block_major:
        outer, inner = groups, blocks
    else:
        outer, inner = blocks, groups
    first, second, slot = row // (outer * CAP), (row // CAP) % outer, row % CAP
    return (col == (second * inner + first) * CAP + slot).astype(f32).astype(bf16)


def chunks_of(start, stop, size):
    return [(at, min(size, stop - at)) for at in range(start, stop, size)]


def loads(pieces, sem):
    copies = [pltpu.make_async_copy(src, dst, sem.at[i]) for i, (src, dst) in enumerate(pieces)]
    for copy in copies:
        copy.start()
    return copies


def up_loads(pieces, base, x_hbm, wg_hbm, wu_hbm, x_buf, wg_buf, wu_buf):
    out = []
    for at, size in pieces:
        here, there = pl.ds(at - base, size), pl.ds(at, size)
        out.append((x_hbm.at[:, here], x_buf.at[:, here]))
        out.append((wg_hbm.at[0, there, :], wg_buf.at[here, :]))
        out.append((wu_hbm.at[0, there, :], wu_buf.at[here, :]))
    return out


def up_sums(pieces, base, copies, x_buf, wg_buf, wu_buf, acc):
    ff = wg_buf.shape[1]
    for i, (at, size) in enumerate(pieces):
        for copy in copies[3 * i : 3 * i + 3]:
            copy.wait()
        here = pl.ds(at - base, size)
        x = x_buf[:, here]
        gate, up = dot(x, wg_buf[here, :]), dot(x, wu_buf[here, :])
        if i == 0:
            acc[:, :ff] = gate
            acc[:, ff:] = up
        else:
            acc[:, :ff] += gate
            acc[:, ff:] += up


def up_first_body(blocks, groups, base, x_hbm, wg_hbm, wu_hbm, part_ref, x_buf, wg_buf, wu_buf, acc, sem):
    pieces = chunks_of(base, wg_hbm.shape[1], UP_CHUNK)
    copies = loads(up_loads(pieces, base, x_hbm, wg_hbm, wu_hbm, x_buf, wg_buf, wu_buf), sem)
    order = reorder(acc.shape[0], blocks, groups, True)
    up_sums(pieces, base, copies, x_buf, wg_buf, wu_buf, acc)
    hi, mid, lo = split3(acc[...])
    part_ref[...] = dot(order, hi) + dot(order, mid) + dot(order, lo)


def up_first(x, w_gate, w_up, blocks, groups):
    slots, width = x.shape
    _, total, ff = w_gate.shape
    copies = 3 * len(chunks_of(total - width, total, UP_CHUNK))
    return pl.pallas_call(
        functools.partial(up_first_body, blocks, groups, total - width),
        in_specs=[pl.BlockSpec(memory_space=pl.ANY)] + [pl.BlockSpec(memory_space=pltpu.HBM)] * 2,
        out_shape=jax.ShapeDtypeStruct((slots, 2 * ff), f32),
        scratch_shapes=[
            pltpu.VMEM((slots, width), bf16),
            pltpu.VMEM((width, ff), bf16),
            pltpu.VMEM((width, ff), bf16),
            pltpu.VMEM((slots, 2 * ff), f32),
            pltpu.SemaphoreType.DMA((copies,)),
        ],
        compiler_params=params(),
        cost_estimate=pl.CostEstimate(
            flops=4 * slots * width * ff, bytes_accessed=2 * width * (slots + 2 * ff), transcendentals=0
        ),
        name="up_first",
    )(x, w_gate, w_up)


def rest_body(part_hbm, x_hbm, wg_hbm, wu_hbm, wd_hbm, y_hbm, act_ref, *scratch):
    part_buf, x_buf, wg_buf, wu_buf, wd_buf, y_buf, acc, sem, y_sem = scratch
    slots, width = x_hbm.shape
    ff = wg_hbm.shape[2]
    pieces = chunks_of(0, width, UP_CHUNK)
    back = y_hbm.shape[1]
    downs = chunks_of(0, back, DOWN_CHUNK)
    wanted = up_loads(pieces, 0, x_hbm, wg_hbm, wu_hbm, x_buf, wg_buf, wu_buf)
    wanted.append((part_hbm, part_buf))
    wanted.append((wd_hbm.at[0, :, pl.ds(0, back)], wd_buf))
    copies = loads(wanted, sem)
    up_sums(pieces, 0, copies, x_buf, wg_buf, wu_buf, acc)
    copies[-2].wait()
    gate = acc[:, :ff] + part_buf[:, :ff]
    up = acc[:, ff:] + part_buf[:, ff:]
    act = (gate / (1.0 + jnp.exp(-gate)) * up).astype(bf16)
    act_ref[...] = act
    copies[-1].wait()
    out = []
    for i, (at, size) in enumerate(downs):
        here = pl.ds(at, size)
        y_buf[:, here] = dot(act_ref[...], wd_buf[:, here]).astype(bf16)
        copy = pltpu.make_async_copy(y_buf.at[:, here], y_hbm.at[:, here], y_sem.at[i])
        copy.start()
        out.append(copy)
    for copy in out:
        copy.wait()


def up_rest_down(part, x, w_gate, w_up, w_down, back):
    slots, width = x.shape
    ff = w_gate.shape[2]
    copies = 3 * len(chunks_of(0, width, UP_CHUNK)) + 2
    return pl.pallas_call(
        rest_body,
        in_specs=[pl.BlockSpec(memory_space=pl.ANY)] + [pl.BlockSpec(memory_space=pltpu.HBM)] * 4,
        out_specs=[pl.BlockSpec(memory_space=pltpu.HBM), pl.BlockSpec(memory_space=pltpu.VMEM)],
        out_shape=(pltpu.HBM((slots, back), bf16), jax.ShapeDtypeStruct((slots, ff), bf16)),
        scratch_shapes=[
            pltpu.VMEM((slots, 2 * ff), f32),
            pltpu.VMEM((slots, width), bf16),
            pltpu.VMEM((width, ff), bf16),
            pltpu.VMEM((width, ff), bf16),
            pltpu.VMEM((ff, back), bf16),
            pltpu.VMEM((slots, back), bf16),
            pltpu.VMEM((slots, 2 * ff), f32),
            pltpu.SemaphoreType.DMA((copies,)),
            pltpu.SemaphoreType.DMA((len(chunks_of(0, back, DOWN_CHUNK)),)),
        ],
        compiler_params=params(),
        cost_estimate=pl.CostEstimate(
            flops=6 * slots * width * ff, bytes_accessed=2 * width * (2 * slots + 3 * ff), transcendentals=slots * ff
        ),
        name="up_rest_down",
    )(part, x, w_gate, w_up, w_down)


def down_body(blocks, groups, act_ref, wd_hbm, out_ref, wd_buf, act_buf, sem):
    slots, width = out_ref.shape
    base = wd_hbm.shape[2] - width
    downs = chunks_of(0, width, DOWN_CHUNK)
    copies = loads([(wd_hbm.at[0, :, pl.ds(base + at, size)], wd_buf.at[:, pl.ds(at, size)]) for at, size in downs], sem)
    act_buf[...] = dot(reorder(slots, blocks, groups, False), act_ref[...]).astype(bf16)
    for copy, (at, size) in zip(copies, downs):
        copy.wait()
        out_ref[:, pl.ds(at, size)] = dot(act_buf[...], wd_buf[:, pl.ds(at, size)]).astype(bf16)


def down(act, w_down, width, blocks, groups):
    slots, ff = act.shape
    return pl.pallas_call(
        functools.partial(down_body, blocks, groups),
        in_specs=[pl.BlockSpec(memory_space=pltpu.VMEM), pl.BlockSpec(memory_space=pltpu.HBM)],
        out_shape=jax.ShapeDtypeStruct((slots, width), bf16),
        scratch_shapes=[
            pltpu.VMEM((ff, width), bf16),
            pltpu.VMEM((slots, ff), bf16),
            pltpu.SemaphoreType.DMA((len(chunks_of(0, width, DOWN_CHUNK)),)),
        ],
        compiler_params=params(),
        cost_estimate=pl.CostEstimate(
            flops=2 * slots * width * ff, bytes_accessed=2 * width * (slots + ff), transcendentals=0
        ),
        name="down",
    )(act, w_down)


def local(attn_parts, residual, norm_gain, router_weight, expert_ids, w_gate, w_up, w_down):
    blocks = lax.axis_size("grp")
    dp_count = lax.axis_size("dp")
    groups = lax.axis_size("role") * dp_count
    plane = ("role", "dp")
    rows_dev, width = residual.shape
    experts = router_weight.shape[1]
    top = expert_ids.shape[1]
    cb, cb_back = B_OUT, B_BACK
    ca, ca_back = width - cb, width - cb_back
    rows_pad = 8

    part = attn_parts[0]
    col_width = part.shape[1]
    tiles = -(-col_width // 128)
    pieces = jnp.pad(part, ((0, 0), (0, tiles * 128 - col_width)))
    pieces = pieces.reshape(blocks * dp_count, rows_dev * tiles, 128)
    received = lax.all_to_all(pieces, ("grp", "dp"), split_axis=0, concat_axis=0, tiled=True)
    received = received.reshape(blocks, dp_count, rows_dev * tiles, 128)
    attention = jnp.sum(received.astype(f32), axis=0)
    attention = attention.reshape(dp_count, rows_dev, tiles * 128)[:, :, :col_width]
    attention = attention.transpose(1, 0, 2).reshape(rows_dev, width)
    hidden = (residual.astype(f32) + attention).astype(bf16)
    hidden = jnp.pad(hidden, ((0, rows_pad - rows_dev), (0, 0)))

    ids = jnp.pad(expert_ids, ((0, rows_pad - rows_dev), (0, 0)), constant_values=int(NO_EXPERT))
    out_a, payload, comb_a = route(hidden, norm_gain[None], router_weight.T, ids, rows_dev, ca)

    arrived = lax.all_to_all(out_a.reshape(groups, CAP, ca), plane, split_axis=0, concat_axis=0, tiled=True)
    arrived = arrived.reshape(groups * CAP, ca)
    arrived, payload = lax.optimization_barrier((arrived, payload))
    x_a = lax.all_gather(arrived, "grp", axis=0, tiled=True)

    payload = payload[:rows_dev].reshape(-1, 128)
    copies = jnp.broadcast_to(payload[None], (blocks,) + payload.shape)
    column = lax.all_to_all(copies, "grp", split_axis=0, concat_axis=0, tiled=True)
    out_b, comb_b = spread_rows(column.reshape(blocks * rows_dev, cb + AUX), top, experts, rows_dev)
    x_b = lax.all_to_all(out_b.reshape(groups, blocks * CAP, cb), plane, split_axis=0, concat_axis=0, tiled=True)
    x_b = x_b.reshape(groups * blocks * CAP, cb)

    w_gate, w_up, w_down, x_a = (
        pltpu.with_memory_space_constraint(w, pltpu.HBM) for w in (w_gate, w_up, w_down, x_a)
    )
    part_up = up_first(x_b, w_gate, w_up, blocks, groups)
    y_a, act = up_rest_down(part_up, x_a, w_gate, w_up, w_down, ca_back)
    sum_a = lax.psum_scatter(y_a, "grp", scatter_dimension=0, tiled=True)

    y_b = down(act, w_down, cb_back, blocks, groups)
    back_b = lax.all_to_all(y_b.reshape(groups, blocks * CAP, cb_back), plane, split_axis=0, concat_axis=0, tiled=True)
    mixed_b = dot(comb_b, back_b.reshape(groups * blocks * CAP, cb_back))
    mixed_b = (mixed_b[: blocks * rows_dev] + mixed_b[blocks * rows_dev :]).astype(bf16)
    mixed_b = mixed_b.reshape(blocks, -1, 128)
    mixed_b = lax.all_to_all(mixed_b, "grp", split_axis=0, concat_axis=0, tiled=True)
    routed_b = jnp.sum(mixed_b.astype(f32), axis=0).reshape(rows_dev, cb_back)

    sum_a, routed_b = lax.optimization_barrier((sum_a, routed_b))
    back_a = lax.all_to_all(sum_a.reshape(groups, CAP, ca_back), plane, split_axis=0, concat_axis=0, tiled=True)
    routed_a = dot(comb_a.astype(bf16), back_a.reshape(groups * CAP, ca_back))
    routed_a = routed_a[:rows_dev] + routed_a[rows_pad : rows_pad + rows_dev]
    routed = jnp.concatenate([routed_a, routed_b], axis=1)
    return (hidden[:rows_dev].astype(f32) + routed).astype(bf16)


def solution(mesh):
    in_specs = (
        P("grp", "role", "dp"),
        P(("role", "grp", "dp"), None),
        P(),
        P(),
        P(("role", "grp", "dp"), None),
        P(("role", "dp"), None, "grp"),
        P(("role", "dp"), None, "grp"),
        P(("role", "dp"), "grp", None),
    )
    out_specs = P(("role", "grp", "dp"), None)
    return jax.shard_map(local, mesh=mesh, in_specs=in_specs, out_specs=out_specs, check_vma=False)
```

```python
import functools

import jax
import jax.numpy as jnp
from jax import lax
from jax.experimental import pallas as pl
from jax.experimental.pallas import tpu as pltpu
from jax.sharding import PartitionSpec as P

CAP = 2
B_OUT = 2560
B_BACK = 2688
UP_CHUNK = 1024
DOWN_CHUNK = 1024
VMEM_MIB = 40
AUX = 128
NO_EXPERT = 99.0

norm_eps = 1e-06
route_scale = 2.5
f32 = jnp.float32
bf16 = jnp.bfloat16


def iota(shape, dim):
    return lax.broadcasted_iota(jnp.int32, shape, dim)


def dot(a, b, contract=((1,), (0,))):
    return lax.dot_general(a, b, (contract, ((), ())), preferred_element_type=f32)


def split3(x):
    hi = x.astype(bf16)
    rest = x - hi.astype(f32)
    mid = rest.astype(bf16)
    lo = (rest - mid.astype(f32)).astype(bf16)
    return hi, mid, lo


def params():
    return pltpu.CompilerParams(vmem_limit_bytes=VMEM_MIB * 1024 * 1024)


def slots_of(ids, weight_cols, rows, rows_block, experts, per_expert_cols):
    blocks = rows // rows_block
    lane = iota((rows, experts), 1).astype(f32)
    chosen = jnp.zeros((rows, experts), f32)
    per_expert = jnp.zeros((rows, experts), f32)
    for k in range(len(weight_cols)):
        match = (ids[:, k : k + 1] == lane).astype(f32)
        chosen = chosen + match
        per_expert = per_expert + match * weight_cols[k]
    r, c = iota((rows, rows), 0), iota((rows, rows), 1)
    before = ((r // rows_block == c // rows_block) & (c < r)).astype(f32).astype(bf16)
    rank = dot(before, chosen.astype(bf16))
    cols = experts * per_expert_cols
    spread = (iota((experts, cols), 1) // per_expert_cols == iota((experts, cols), 0)).astype(f32).astype(bf16)
    hi, mid, lo = split3(per_expert)
    chosen_x = dot(chosen.astype(bf16), spread)
    rank_x = dot(rank.astype(bf16), spread)
    weight_x = dot(hi, spread) + dot(mid, spread) + dot(lo, spread)
    col = iota((rows, cols), 1)
    own = (col // CAP) % blocks == iota((rows, cols), 0) // rows_block
    select = jnp.where(own & (rank_x == (col % CAP).astype(f32)), chosen_x, 0.0)
    return select, select * weight_x


def route_body(rows_dev, top, experts, ca, hidden_ref, gain_ref, router_ref, ids_ref, out_ref, payload_ref, comb_ref):
    h = hidden_ref[...].astype(f32)
    rows, width = h.shape
    meansq = jnp.sum(h * h, axis=-1, keepdims=True) * (1.0 / width)
    normed = (h * lax.rsqrt(meansq + norm_eps) * gain_ref[...].astype(f32)).astype(bf16)
    scores = jax.nn.sigmoid(dot(normed, router_ref[...], ((1,), (1,))))
    ids = ids_ref[...].astype(f32)
    lane = iota((rows, experts), 1).astype(f32)
    picked = [
        jnp.sum(jnp.where(ids[:, k : k + 1] == lane, scores, 0.0), axis=-1, keepdims=True) for k in range(top)
    ]
    total = functools.reduce(lambda a, b: a + b, picked)
    total = jnp.where(iota((rows, 1), 0) < rows_dev, total, 1.0)
    weights = [route_scale * p / total for p in picked]
    select, combine = slots_of(ids, weights, rows, rows, experts, CAP)
    hi, mid, _ = split3(combine)
    comb_ref[:rows, :] = hi.astype(f32)
    comb_ref[rows:, :] = mid.astype(f32)
    out_ref[...] = dot(select.astype(bf16), normed[:, :ca], ((0,), (0,))).astype(bf16)
    payload_ref[:, : width - ca] = normed[:, ca:]
    at = iota((rows, AUX), 1)
    aux = jnp.zeros((rows, AUX), f32)
    for k in range(top):
        aux = jnp.where(at == k, ids[:, k : k + 1], aux)
        for part, value in enumerate(split3(weights[k])):
            aux = jnp.where(at == (part + 1) * top + k, value.astype(f32), aux)
    payload_ref[:, width - ca :] = aux.astype(bf16)


def route(hidden, gain, router_t, ids, rows_dev, ca):
    rows, width = hidden.shape
    experts, top = router_t.shape[0], ids.shape[1]
    return pl.pallas_call(
        functools.partial(route_body, rows_dev, top, experts, ca),
        out_shape=(
            jax.ShapeDtypeStruct((experts * CAP, ca), bf16),
            jax.ShapeDtypeStruct((rows, width - ca + AUX), bf16),
            jax.ShapeDtypeStruct((2 * rows, experts * CAP), f32),
        ),
        compiler_params=params(),
        name="route",
    )(hidden, gain, router_t, ids)


def spread_body(top, experts, rows_block, rows_ref, out_ref, comb_ref):
    rows = rows_ref.shape[0]
    blocks = rows // rows_block
    cb = rows_ref.shape[1] - AUX
    aux = rows_ref[:, cb:].astype(f32)
    ids = aux[:, :top]
    weights = [
        aux[:, top + k : top + k + 1] + aux[:, 2 * top + k : 2 * top + k + 1] + aux[:, 3 * top + k : 3 * top + k + 1]
        for k in range(top)
    ]
    select, combine = slots_of(ids, weights, rows, rows_block, experts, blocks * CAP)
    hi, mid, _ = split3(combine)
    comb_ref[:rows, :] = hi
    comb_ref[rows:, :] = mid
    out_ref[...] = dot(select.astype(bf16), rows_ref[:, :cb], ((0,), (0,))).astype(bf16)


def spread_rows(rows_in, top, experts, rows_block):
    rows, width = rows_in.shape
    slots = experts * (rows // rows_block) * CAP
    return pl.pallas_call(
        functools.partial(spread_body, top, experts, rows_block),
        out_shape=(
            jax.ShapeDtypeStruct((slots, width - AUX), bf16),
            jax.ShapeDtypeStruct((2 * rows, slots), bf16),
        ),
        compiler_params=params(),
        name="spread_rows",
    )(rows_in)


def reorder(slots, blocks, groups, to_block_major):
    row, col = iota((slots, slots), 0), iota((slots, slots), 1)
    if to_block_major:
        outer, inner = groups, blocks
    else:
        outer, inner = blocks, groups
    first, second, slot = row // (outer * CAP), (row // CAP) % outer, row % CAP
    return (col == (second * inner + first) * CAP + slot).astype(f32).astype(bf16)


def chunks_of(start, stop, size):
    return [(at, min(size, stop - at)) for at in range(start, stop, size)]


def loads(pieces, sem):
    copies = [pltpu.make_async_copy(src, dst, sem.at[i]) for i, (src, dst) in enumerate(pieces)]
    for copy in copies:
        copy.start()
    return copies


def up_loads(pieces, base, x_hbm, wg_hbm, wu_hbm, x_buf, wg_buf, wu_buf):
    out = []
    for at, size in pieces:
        here, there = pl.ds(at - base, size), pl.ds(at, size)
        out.append((x_hbm.at[:, here], x_buf.at[:, here]))
        out.append((wg_hbm.at[0, there, :], wg_buf.at[here, :]))
        out.append((wu_hbm.at[0, there, :], wu_buf.at[here, :]))
    return out


def up_sums(pieces, base, copies, x_buf, wg_buf, wu_buf, acc):
    ff = wg_buf.shape[1]
    for i, (at, size) in enumerate(pieces):
        for copy in copies[3 * i : 3 * i + 3]:
            copy.wait()
        here = pl.ds(at - base, size)
        x = x_buf[:, here]
        gate, up = dot(x, wg_buf[here, :]), dot(x, wu_buf[here, :])
        if i == 0:
            acc[:, :ff] = gate
            acc[:, ff:] = up
        else:
            acc[:, :ff] += gate
            acc[:, ff:] += up


def up_first_body(blocks, groups, base, x_ref, wg_hbm, wu_hbm, part_ref, wg_buf, wu_buf, acc, sem):
    pieces = chunks_of(base, wg_hbm.shape[1], UP_CHUNK)
    ff = wg_buf.shape[1]
    wanted = []
    for at, size in pieces:
        here, there = pl.ds(at - base, size), pl.ds(at, size)
        wanted.append((wg_hbm.at[0, there, :], wg_buf.at[here, :]))
        wanted.append((wu_hbm.at[0, there, :], wu_buf.at[here, :]))
    copies = loads(wanted, sem)
    order = reorder(acc.shape[0], blocks, groups, True)
    for i, (at, size) in enumerate(pieces):
        copies[2 * i].wait()
        copies[2 * i + 1].wait()
        here = pl.ds(at - base, size)
        x = x_ref[:, here]
        gate, up = dot(x, wg_buf[here, :]), dot(x, wu_buf[here, :])
        if i == 0:
            acc[:, :ff] = gate
            acc[:, ff:] = up
        else:
            acc[:, :ff] += gate
            acc[:, ff:] += up
    hi, mid, lo = split3(acc[...])
    part_ref[...] = dot(order, hi) + dot(order, mid) + dot(order, lo)


def up_first(x, w_gate, w_up, blocks, groups):
    slots, width = x.shape
    _, total, ff = w_gate.shape
    copies = 2 * len(chunks_of(total - width, total, UP_CHUNK))
    return pl.pallas_call(
        functools.partial(up_first_body, blocks, groups, total - width),
        in_specs=[pl.BlockSpec(memory_space=pltpu.VMEM)] + [pl.BlockSpec(memory_space=pltpu.HBM)] * 2,
        out_shape=jax.ShapeDtypeStruct((slots, 2 * ff), f32),
        scratch_shapes=[
            pltpu.VMEM((width, ff), bf16),
            pltpu.VMEM((width, ff), bf16),
            pltpu.VMEM((slots, 2 * ff), f32),
            pltpu.SemaphoreType.DMA((copies,)),
        ],
        compiler_params=params(),
        cost_estimate=pl.CostEstimate(
            flops=4 * slots * width * ff, bytes_accessed=2 * width * (slots + 2 * ff), transcendentals=0
        ),
        name="up_first",
    )(x, w_gate, w_up)


def rest_body(part_hbm, x_hbm, wg_hbm, wu_hbm, wd_hbm, y_hbm, act_ref, *scratch):
    part_buf, x_buf, wg_buf, wu_buf, wd_buf, y_buf, acc, sem, y_sem = scratch
    slots, width = x_hbm.shape
    ff = wg_hbm.shape[2]
    pieces = chunks_of(0, width, UP_CHUNK)
    back = y_hbm.shape[1]
    downs = chunks_of(0, back, DOWN_CHUNK)
    wanted = up_loads(pieces, 0, x_hbm, wg_hbm, wu_hbm, x_buf, wg_buf, wu_buf)
    wanted.append((part_hbm, part_buf))
    wanted.append((wd_hbm.at[0, :, pl.ds(0, back)], wd_buf))
    copies = loads(wanted, sem)
    up_sums(pieces, 0, copies, x_buf, wg_buf, wu_buf, acc)
    copies[-2].wait()
    gate = acc[:, :ff] + part_buf[:, :ff]
    up = acc[:, ff:] + part_buf[:, ff:]
    act = (gate / (1.0 + jnp.exp(-gate)) * up).astype(bf16)
    act_ref[...] = act
    copies[-1].wait()
    out = []
    for i, (at, size) in enumerate(downs):
        here = pl.ds(at, size)
        y_buf[:, here] = dot(act_ref[...], wd_buf[:, here]).astype(bf16)
        copy = pltpu.make_async_copy(y_buf.at[:, here], y_hbm.at[:, here], y_sem.at[i])
        copy.start()
        out.append(copy)
    for copy in out:
        copy.wait()


def up_rest_down(part, x, w_gate, w_up, w_down, back):
    slots, width = x.shape
    ff = w_gate.shape[2]
    copies = 3 * len(chunks_of(0, width, UP_CHUNK)) + 2
    return pl.pallas_call(
        rest_body,
        in_specs=[pl.BlockSpec(memory_space=pl.ANY)] + [pl.BlockSpec(memory_space=pltpu.HBM)] * 4,
        out_specs=[pl.BlockSpec(memory_space=pltpu.HBM), pl.BlockSpec(memory_space=pltpu.VMEM)],
        out_shape=(pltpu.HBM((slots, back), bf16), jax.ShapeDtypeStruct((slots, ff), bf16)),
        scratch_shapes=[
            pltpu.VMEM((slots, 2 * ff), f32),
            pltpu.VMEM((slots, width), bf16),
            pltpu.VMEM((width, ff), bf16),
            pltpu.VMEM((width, ff), bf16),
            pltpu.VMEM((ff, back), bf16),
            pltpu.VMEM((slots, back), bf16),
            pltpu.VMEM((slots, 2 * ff), f32),
            pltpu.SemaphoreType.DMA((copies,)),
            pltpu.SemaphoreType.DMA((len(chunks_of(0, back, DOWN_CHUNK)),)),
        ],
        compiler_params=params(),
        cost_estimate=pl.CostEstimate(
            flops=6 * slots * width * ff, bytes_accessed=2 * width * (2 * slots + 3 * ff), transcendentals=slots * ff
        ),
        name="up_rest_down",
    )(part, x, w_gate, w_up, w_down)


def down_body(blocks, groups, act_ref, wd_hbm, out_ref, wd_buf, act_buf, sem):
    slots, width = out_ref.shape
    base = wd_hbm.shape[2] - width
    downs = chunks_of(0, width, DOWN_CHUNK)
    copies = loads([(wd_hbm.at[0, :, pl.ds(base + at, size)], wd_buf.at[:, pl.ds(at, size)]) for at, size in downs], sem)
    act_buf[...] = dot(reorder(slots, blocks, groups, False), act_ref[...]).astype(bf16)
    for copy, (at, size) in zip(copies, downs):
        copy.wait()
        out_ref[:, pl.ds(at, size)] = dot(act_buf[...], wd_buf[:, pl.ds(at, size)]).astype(bf16)


def down(act, w_down, width, blocks, groups):
    slots, ff = act.shape
    return pl.pallas_call(
        functools.partial(down_body, blocks, groups),
        in_specs=[pl.BlockSpec(memory_space=pltpu.VMEM), pl.BlockSpec(memory_space=pltpu.HBM)],
        out_shape=jax.ShapeDtypeStruct((slots, width), bf16),
        scratch_shapes=[
            pltpu.VMEM((ff, width), bf16),
            pltpu.VMEM((slots, ff), bf16),
            pltpu.SemaphoreType.DMA((len(chunks_of(0, width, DOWN_CHUNK)),)),
        ],
        compiler_params=params(),
        cost_estimate=pl.CostEstimate(
            flops=2 * slots * width * ff, bytes_accessed=2 * width * (slots + ff), transcendentals=0
        ),
        name="down",
    )(act, w_down)


def local(attn_parts, residual, norm_gain, router_weight, expert_ids, w_gate, w_up, w_down):
    blocks = lax.axis_size("grp")
    dp_count = lax.axis_size("dp")
    groups = lax.axis_size("role") * dp_count
    plane = ("role", "dp")
    rows_dev, width = residual.shape
    experts = router_weight.shape[1]
    top = expert_ids.shape[1]
    cb, cb_back = B_OUT, B_BACK
    ca, ca_back = width - cb, width - cb_back
    rows_pad = 8

    part = attn_parts[0]
    col_width = part.shape[1]
    tiles = -(-col_width // 128)
    pieces = jnp.pad(part, ((0, 0), (0, tiles * 128 - col_width)))
    pieces = pieces.reshape(blocks * dp_count, rows_dev * tiles, 128)
    received = lax.all_to_all(pieces, ("grp", "dp"), split_axis=0, concat_axis=0, tiled=True)
    received = received.reshape(blocks, dp_count, rows_dev * tiles, 128)
    attention = jnp.sum(received.astype(f32), axis=0)
    attention = attention.reshape(dp_count, rows_dev, tiles * 128)[:, :, :col_width]
    attention = attention.transpose(1, 0, 2).reshape(rows_dev, width)
    hidden = (residual.astype(f32) + attention).astype(bf16)
    hidden = jnp.pad(hidden, ((0, rows_pad - rows_dev), (0, 0)))

    ids = jnp.pad(expert_ids, ((0, rows_pad - rows_dev), (0, 0)), constant_values=int(NO_EXPERT))
    out_a, payload, comb_a = route(hidden, norm_gain[None], router_weight.T, ids, rows_dev, ca)

    arrived = lax.all_to_all(out_a.reshape(groups, CAP, ca), plane, split_axis=0, concat_axis=0, tiled=True)
    arrived = arrived.reshape(groups * CAP, ca)
    arrived, payload = lax.optimization_barrier((arrived, payload))
    x_a = lax.all_gather(arrived, "grp", axis=0, tiled=True)

    payload = payload[:rows_dev].reshape(-1, 128)
    copies = jnp.broadcast_to(payload[None], (blocks,) + payload.shape)
    column = lax.all_to_all(copies, "grp", split_axis=0, concat_axis=0, tiled=True)
    out_b, comb_b = spread_rows(column.reshape(blocks * rows_dev, cb + AUX), top, experts, rows_dev)
    x_b = lax.all_to_all(out_b.reshape(groups, blocks * CAP, cb), plane, split_axis=0, concat_axis=0, tiled=True)
    x_b = x_b.reshape(groups * blocks * CAP, cb)

    w_gate, w_up, w_down, x_a = (
        pltpu.with_memory_space_constraint(w, pltpu.HBM) for w in (w_gate, w_up, w_down, x_a)
    )
    part_up = up_first(x_b, w_gate, w_up, blocks, groups)
    y_a, act = up_rest_down(part_up, x_a, w_gate, w_up, w_down, ca_back)
    sum_a = lax.psum_scatter(y_a, "grp", scatter_dimension=0, tiled=True)

    y_b = down(act, w_down, cb_back, blocks, groups)
    back_b = lax.all_to_all(y_b.reshape(groups, blocks * CAP, cb_back), plane, split_axis=0, concat_axis=0, tiled=True)
    mixed_b = dot(comb_b, back_b.reshape(groups * blocks * CAP, cb_back))
    mixed_b = (mixed_b[: blocks * rows_dev] + mixed_b[blocks * rows_dev :]).astype(bf16)
    mixed_b = mixed_b.reshape(blocks, -1, 128)
    mixed_b = lax.all_to_all(mixed_b, "grp", split_axis=0, concat_axis=0, tiled=True)
    routed_b = jnp.sum(mixed_b.astype(f32), axis=0).reshape(rows_dev, cb_back)

    sum_a, routed_b = lax.optimization_barrier((sum_a, routed_b))
    back_a = lax.all_to_all(sum_a.reshape(groups, CAP, ca_back), plane, split_axis=0, concat_axis=0, tiled=True)
    routed_a = dot(comb_a.astype(bf16), back_a.reshape(groups * CAP, ca_back))
    routed_a = routed_a[:rows_dev] + routed_a[rows_pad : rows_pad + rows_dev]
    routed = jnp.concatenate([routed_a, routed_b], axis=1)
    return (hidden[:rows_dev].astype(f32) + routed).astype(bf16)


def solution(mesh):
    in_specs = (
        P("grp", "role", "dp"),
        P(("role", "grp", "dp"), None),
        P(),
        P(),
        P(("role", "grp", "dp"), None),
        P(("role", "dp"), None, "grp"),
        P(("role", "dp"), None, "grp"),
        P(("role", "dp"), "grp", None),
    )
    out_specs = P(("role", "grp", "dp"), None)
    return jax.shard_map(local, mesh=mesh, in_specs=in_specs, out_specs=out_specs, check_vma=False)
```

```python
import functools

import jax
import jax.numpy as jnp
from jax import lax
from jax.experimental import pallas as pl
from jax.experimental.pallas import tpu as pltpu
from jax.sharding import PartitionSpec as P

CAP = 2
B_OUT = 2560
B_BACK = 2688
UP_CHUNK = 1024
DOWN_CHUNK = 1024
VMEM_MIB = 40
AUX = 128
NO_EXPERT = 99.0

norm_eps = 1e-06
route_scale = 2.5
f32 = jnp.float32
bf16 = jnp.bfloat16


def iota(shape, dim):
    return lax.broadcasted_iota(jnp.int32, shape, dim)


def dot(a, b, contract=((1,), (0,))):
    return lax.dot_general(a, b, (contract, ((), ())), preferred_element_type=f32)


def split3(x):
    hi = x.astype(bf16)
    rest = x - hi.astype(f32)
    mid = rest.astype(bf16)
    lo = (rest - mid.astype(f32)).astype(bf16)
    return hi, mid, lo


def params():
    return pltpu.CompilerParams(vmem_limit_bytes=VMEM_MIB * 1024 * 1024)


def slots_of(ids, weight_cols, rows, rows_block, experts, per_expert_cols):
    blocks = rows // rows_block
    lane = iota((rows, experts), 1).astype(f32)
    chosen = jnp.zeros((rows, experts), f32)
    per_expert = jnp.zeros((rows, experts), f32)
    for k in range(len(weight_cols)):
        match = (ids[:, k : k + 1] == lane).astype(f32)
        chosen = chosen + match
        per_expert = per_expert + match * weight_cols[k]
    r, c = iota((rows, rows), 0), iota((rows, rows), 1)
    before = ((r // rows_block == c // rows_block) & (c < r)).astype(f32).astype(bf16)
    rank = dot(before, chosen.astype(bf16))
    cols = experts * per_expert_cols
    spread = (iota((experts, cols), 1) // per_expert_cols == iota((experts, cols), 0)).astype(f32).astype(bf16)
    hi, mid, lo = split3(per_expert)
    chosen_x = dot(chosen.astype(bf16), spread)
    rank_x = dot(rank.astype(bf16), spread)
    weight_x = dot(hi, spread) + dot(mid, spread) + dot(lo, spread)
    col = iota((rows, cols), 1)
    own = (col // CAP) % blocks == iota((rows, cols), 0) // rows_block
    select = jnp.where(own & (rank_x == (col % CAP).astype(f32)), chosen_x, 0.0)
    return select, select * weight_x


def route_body(rows_dev, top, experts, ca, hidden_ref, gain_ref, router_ref, ids_ref, out_ref, payload_ref, comb_ref):
    h = hidden_ref[...].astype(f32)
    rows, width = h.shape
    meansq = jnp.sum(h * h, axis=-1, keepdims=True) * (1.0 / width)
    normed = (h * lax.rsqrt(meansq + norm_eps) * gain_ref[...].astype(f32)).astype(bf16)
    scores = jax.nn.sigmoid(dot(normed, router_ref[...], ((1,), (1,))))
    ids = ids_ref[...].astype(f32)
    lane = iota((rows, experts), 1).astype(f32)
    picked = [
        jnp.sum(jnp.where(ids[:, k : k + 1] == lane, scores, 0.0), axis=-1, keepdims=True) for k in range(top)
    ]
    total = functools.reduce(lambda a, b: a + b, picked)
    total = jnp.where(iota((rows, 1), 0) < rows_dev, total, 1.0)
    weights = [route_scale * p / total for p in picked]
    select, combine = slots_of(ids, weights, rows, rows, experts, CAP)
    hi, mid, _ = split3(combine)
    comb_ref[:rows, :] = hi.astype(f32)
    comb_ref[rows:, :] = mid.astype(f32)
    out_ref[...] = dot(select.astype(bf16), normed[:, :ca], ((0,), (0,))).astype(bf16)
    payload_ref[:, : width - ca] = normed[:, ca:]
    at = iota((rows, AUX), 1)
    aux = jnp.zeros((rows, AUX), f32)
    for k in range(top):
        aux = jnp.where(at == k, ids[:, k : k + 1], aux)
        for part, value in enumerate(split3(weights[k])):
            aux = jnp.where(at == (part + 1) * top + k, value.astype(f32), aux)
    payload_ref[:, width - ca :] = aux.astype(bf16)


def route(hidden, gain, router_t, ids, rows_dev, ca):
    rows, width = hidden.shape
    experts, top = router_t.shape[0], ids.shape[1]
    return pl.pallas_call(
        functools.partial(route_body, rows_dev, top, experts, ca),
        out_shape=(
            jax.ShapeDtypeStruct((experts * CAP, ca), bf16),
            jax.ShapeDtypeStruct((rows, width - ca + AUX), bf16),
            jax.ShapeDtypeStruct((2 * rows, experts * CAP), f32),
        ),
        compiler_params=params(),
        name="route",
    )(hidden, gain, router_t, ids)


def spread_body(top, experts, rows_block, rows_ref, out_ref, comb_ref):
    rows = rows_ref.shape[0]
    blocks = rows // rows_block
    cb = rows_ref.shape[1] - AUX
    aux = rows_ref[:, cb:].astype(f32)
    ids = aux[:, :top]
    weights = [
        aux[:, top + k : top + k + 1] + aux[:, 2 * top + k : 2 * top + k + 1] + aux[:, 3 * top + k : 3 * top + k + 1]
        for k in range(top)
    ]
    select, combine = slots_of(ids, weights, rows, rows_block, experts, blocks * CAP)
    hi, mid, _ = split3(combine)
    comb_ref[:rows, :] = hi
    comb_ref[rows:, :] = mid
    out_ref[...] = dot(select.astype(bf16), rows_ref[:, :cb], ((0,), (0,))).astype(bf16)


def spread_rows(rows_in, top, experts, rows_block):
    rows, width = rows_in.shape
    slots = experts * (rows // rows_block) * CAP
    return pl.pallas_call(
        functools.partial(spread_body, top, experts, rows_block),
        out_shape=(
            jax.ShapeDtypeStruct((slots, width - AUX), bf16),
            jax.ShapeDtypeStruct((2 * rows, slots), bf16),
        ),
        compiler_params=params(),
        name="spread_rows",
    )(rows_in)


def reorder(slots, blocks, groups, to_block_major):
    row, col = iota((slots, slots), 0), iota((slots, slots), 1)
    if to_block_major:
        outer, inner = groups, blocks
    else:
        outer, inner = blocks, groups
    first, second, slot = row // (outer * CAP), (row // CAP) % outer, row % CAP
    return (col == (second * inner + first) * CAP + slot).astype(f32).astype(bf16)


def chunks_of(start, stop, size):
    return [(at, min(size, stop - at)) for at in range(start, stop, size)]


def loads(pieces, sem):
    copies = [pltpu.make_async_copy(src, dst, sem.at[i]) for i, (src, dst) in enumerate(pieces)]
    for copy in copies:
        copy.start()
    return copies


def up_loads(pieces, base, x_hbm, wg_hbm, wu_hbm, x_buf, wg_buf, wu_buf):
    out = []
    for at, size in pieces:
        here, there = pl.ds(at - base, size), pl.ds(at, size)
        out.append((x_hbm.at[:, here], x_buf.at[:, here]))
        out.append((wg_hbm.at[0, there, :], wg_buf.at[here, :]))
        out.append((wu_hbm.at[0, there, :], wu_buf.at[here, :]))
    return out


def up_sums(pieces, base, copies, x_buf, wg_buf, wu_buf, acc):
    ff = wg_buf.shape[1]
    for i, (at, size) in enumerate(pieces):
        for copy in copies[3 * i : 3 * i + 3]:
            copy.wait()
        here = pl.ds(at - base, size)
        x = x_buf[:, here]
        gate, up = dot(x, wg_buf[here, :]), dot(x, wu_buf[here, :])
        if i == 0:
            acc[:, :ff] = gate
            acc[:, ff:] = up
        else:
            acc[:, :ff] += gate
            acc[:, ff:] += up


def up_first_body(blocks, groups, base, x_ref, wg_hbm, wu_hbm, part_ref, wg_buf, wu_buf, acc, sem):
    pieces = chunks_of(base, wg_hbm.shape[1], UP_CHUNK)
    ff = wg_buf.shape[1]
    wanted = []
    for at, size in pieces:
        here, there = pl.ds(at - base, size), pl.ds(at, size)
        wanted.append((wg_hbm.at[0, there, :], wg_buf.at[here, :]))
        wanted.append((wu_hbm.at[0, there, :], wu_buf.at[here, :]))
    copies = loads(wanted, sem)
    order = reorder(acc.shape[0], blocks, groups, True)
    for i, (at, size) in enumerate(pieces):
        copies[2 * i].wait()
        copies[2 * i + 1].wait()
        here = pl.ds(at - base, size)
        x = x_ref[:, here]
        gate, up = dot(x, wg_buf[here, :]), dot(x, wu_buf[here, :])
        if i == 0:
            acc[:, :ff] = gate
            acc[:, ff:] = up
        else:
            acc[:, :ff] += gate
            acc[:, ff:] += up
    hi, mid, lo = split3(acc[...])
    part_ref[...] = dot(order, hi) + dot(order, mid) + dot(order, lo)


def up_first(x, w_gate, w_up, blocks, groups):
    slots, width = x.shape
    _, total, ff = w_gate.shape
    copies = 2 * len(chunks_of(total - width, total, UP_CHUNK))
    return pl.pallas_call(
        functools.partial(up_first_body, blocks, groups, total - width),
        in_specs=[pl.BlockSpec(memory_space=pltpu.VMEM)] + [pl.BlockSpec(memory_space=pltpu.HBM)] * 2,
        out_shape=jax.ShapeDtypeStruct((slots, 2 * ff), f32),
        scratch_shapes=[
            pltpu.VMEM((width, ff), bf16),
            pltpu.VMEM((width, ff), bf16),
            pltpu.VMEM((slots, 2 * ff), f32),
            pltpu.SemaphoreType.DMA((copies,)),
        ],
        compiler_params=params(),
        cost_estimate=pl.CostEstimate(
            flops=4 * slots * width * ff, bytes_accessed=2 * width * (slots + 2 * ff), transcendentals=0
        ),
        name="up_first",
    )(x, w_gate, w_up)


def rest_body(part_hbm, x_hbm, wg_hbm, wu_hbm, wd_hbm, y_hbm, act_ref, *scratch):
    part_buf, x_buf, wg_buf, wu_buf, wd_buf, y_buf, acc, sem, y_sem = scratch
    slots, width = x_hbm.shape
    ff = wg_hbm.shape[2]
    pieces = chunks_of(0, width, UP_CHUNK)
    back = y_hbm.shape[1]
    downs = chunks_of(0, back, DOWN_CHUNK)
    wanted = up_loads(pieces, 0, x_hbm, wg_hbm, wu_hbm, x_buf, wg_buf, wu_buf)
    wanted.append((part_hbm, part_buf))
    wanted.append((wd_hbm.at[0, :, pl.ds(0, back)], wd_buf))
    copies = loads(wanted, sem)
    up_sums(pieces, 0, copies, x_buf, wg_buf, wu_buf, acc)
    copies[-2].wait()
    gate = acc[:, :ff] + part_buf[:, :ff]
    up = acc[:, ff:] + part_buf[:, ff:]
    act = (gate / (1.0 + jnp.exp(-gate)) * up).astype(bf16)
    act_ref[...] = act
    copies[-1].wait()
    out = []
    for i, (at, size) in enumerate(downs):
        here = pl.ds(at, size)
        y_buf[:, here] = dot(act_ref[...], wd_buf[:, here]).astype(bf16)
        copy = pltpu.make_async_copy(y_buf.at[:, here], y_hbm.at[:, here], y_sem.at[i])
        copy.start()
        out.append(copy)
    for copy in out:
        copy.wait()


def up_rest_down(part, x, w_gate, w_up, w_down, back):
    slots, width = x.shape
    ff = w_gate.shape[2]
    copies = 3 * len(chunks_of(0, width, UP_CHUNK)) + 2
    return pl.pallas_call(
        rest_body,
        in_specs=[pl.BlockSpec(memory_space=pl.ANY)] + [pl.BlockSpec(memory_space=pltpu.HBM)] * 4,
        out_specs=[pl.BlockSpec(memory_space=pltpu.HBM), pl.BlockSpec(memory_space=pltpu.VMEM)],
        out_shape=(pltpu.HBM((slots, back), bf16), jax.ShapeDtypeStruct((slots, ff), bf16)),
        scratch_shapes=[
            pltpu.VMEM((slots, 2 * ff), f32),
            pltpu.VMEM((slots, width), bf16),
            pltpu.VMEM((width, ff), bf16),
            pltpu.VMEM((width, ff), bf16),
            pltpu.VMEM((ff, back), bf16),
            pltpu.VMEM((slots, back), bf16),
            pltpu.VMEM((slots, 2 * ff), f32),
            pltpu.SemaphoreType.DMA((copies,)),
            pltpu.SemaphoreType.DMA((len(chunks_of(0, back, DOWN_CHUNK)),)),
        ],
        compiler_params=params(),
        cost_estimate=pl.CostEstimate(
            flops=6 * slots * width * ff, bytes_accessed=2 * width * (2 * slots + 3 * ff), transcendentals=slots * ff
        ),
        name="up_rest_down",
    )(part, x, w_gate, w_up, w_down)


def down_body(blocks, groups, act_ref, wd_hbm, out_ref, wd_buf, act_buf, sem):
    slots, width = out_ref.shape
    base = wd_hbm.shape[2] - width
    downs = chunks_of(0, width, DOWN_CHUNK)
    copies = loads([(wd_hbm.at[0, :, pl.ds(base + at, size)], wd_buf.at[:, pl.ds(at, size)]) for at, size in downs], sem)
    act_buf[...] = dot(reorder(slots, blocks, groups, False), act_ref[...]).astype(bf16)
    for copy, (at, size) in zip(copies, downs):
        copy.wait()
        out_ref[:, pl.ds(at, size)] = dot(act_buf[...], wd_buf[:, pl.ds(at, size)]).astype(bf16)


def down(act, w_down, width, blocks, groups):
    slots, ff = act.shape
    return pl.pallas_call(
        functools.partial(down_body, blocks, groups),
        in_specs=[pl.BlockSpec(memory_space=pltpu.VMEM), pl.BlockSpec(memory_space=pltpu.HBM)],
        out_shape=jax.ShapeDtypeStruct((slots, width), bf16),
        scratch_shapes=[
            pltpu.VMEM((ff, width), bf16),
            pltpu.VMEM((slots, ff), bf16),
            pltpu.SemaphoreType.DMA((len(chunks_of(0, width, DOWN_CHUNK)),)),
        ],
        compiler_params=params(),
        cost_estimate=pl.CostEstimate(
            flops=2 * slots * width * ff, bytes_accessed=2 * width * (slots + ff), transcendentals=0
        ),
        name="down",
    )(act, w_down)


def local(attn_parts, residual, norm_gain, router_weight, expert_ids, w_gate, w_up, w_down):
    blocks = lax.axis_size("grp")
    dp_count = lax.axis_size("dp")
    groups = lax.axis_size("role") * dp_count
    plane = ("role", "dp")
    rows_dev, width = residual.shape
    experts = router_weight.shape[1]
    top = expert_ids.shape[1]
    cb, cb_back = B_OUT, B_BACK
    ca, ca_back = width - cb, width - cb_back
    rows_pad = 8

    part = attn_parts[0]
    col_width = part.shape[1]
    flat = rows_dev * col_width
    pairs = -(-flat // 256)
    pieces = jnp.pad(part.reshape(blocks * dp_count, flat), ((0, 0), (0, pairs * 256 - flat)))
    pieces = pieces.reshape(blocks * dp_count, pairs, 2, 128)
    received = lax.all_to_all(pieces, ("grp", "dp"), split_axis=0, concat_axis=0, tiled=True)
    received = received.reshape(blocks, dp_count, pairs, 2, 128)
    attention = jnp.sum(received.astype(f32), axis=0)
    attention = attention.reshape(dp_count, pairs * 256)[:, :flat].reshape(dp_count, rows_dev, col_width)
    attention = attention.transpose(1, 0, 2).reshape(rows_dev, width)
    hidden = (residual.astype(f32) + attention).astype(bf16)
    hidden = jnp.pad(hidden, ((0, rows_pad - rows_dev), (0, 0)))

    ids = jnp.pad(expert_ids, ((0, rows_pad - rows_dev), (0, 0)), constant_values=int(NO_EXPERT))
    out_a, payload, comb_a = route(hidden, norm_gain[None], router_weight.T, ids, rows_dev, ca)

    arrived = lax.all_to_all(out_a.reshape(groups, CAP, ca), plane, split_axis=0, concat_axis=0, tiled=True)
    arrived = arrived.reshape(groups * CAP, ca)
    arrived, payload = lax.optimization_barrier((arrived, payload))
    x_a = lax.all_gather(arrived, "grp", axis=0, tiled=True)

    payload = payload[:rows_dev].reshape(-1, 128)
    copies = jnp.broadcast_to(payload[None], (blocks,) + payload.shape)
    column = lax.all_to_all(copies, "grp", split_axis=0, concat_axis=0, tiled=True)
    out_b, comb_b = spread_rows(column.reshape(blocks * rows_dev, cb + AUX), top, experts, rows_dev)
    x_b = lax.all_to_all(out_b.reshape(groups, blocks * CAP, cb), plane, split_axis=0, concat_axis=0, tiled=True)
    x_b = x_b.reshape(groups * blocks * CAP, cb)

    w_gate, w_up, w_down, x_a = (
        pltpu.with_memory_space_constraint(w, pltpu.HBM) for w in (w_gate, w_up, w_down, x_a)
    )
    part_up = up_first(x_b, w_gate, w_up, blocks, groups)
    y_a, act = up_rest_down(part_up, x_a, w_gate, w_up, w_down, ca_back)
    sum_a = lax.psum_scatter(y_a, "grp", scatter_dimension=0, tiled=True)

    y_b = down(act, w_down, cb_back, blocks, groups)
    back_b = lax.all_to_all(y_b.reshape(groups, blocks * CAP, cb_back), plane, split_axis=0, concat_axis=0, tiled=True)
    mixed_b = dot(comb_b, back_b.reshape(groups * blocks * CAP, cb_back))
    mixed_b = (mixed_b[: blocks * rows_dev] + mixed_b[blocks * rows_dev :]).astype(bf16)
    mixed_b = mixed_b.reshape(blocks, -1, 128)
    mixed_b = lax.all_to_all(mixed_b, "grp", split_axis=0, concat_axis=0, tiled=True)
    routed_b = jnp.sum(mixed_b.astype(f32), axis=0).reshape(rows_dev, cb_back)

    sum_a, routed_b = lax.optimization_barrier((sum_a, routed_b))
    back_a = lax.all_to_all(sum_a.reshape(groups, CAP, ca_back), plane, split_axis=0, concat_axis=0, tiled=True)
    routed_a = dot(comb_a.astype(bf16), back_a.reshape(groups * CAP, ca_back))
    routed_a = routed_a[:rows_dev] + routed_a[rows_pad : rows_pad + rows_dev]
    routed = jnp.concatenate([routed_a, routed_b], axis=1)
    return (hidden[:rows_dev].astype(f32) + routed).astype(bf16)


def solution(mesh):
    in_specs = (
        P("grp", "role", "dp"),
        P(("role", "grp", "dp"), None),
        P(),
        P(),
        P(("role", "grp", "dp"), None),
        P(("role", "dp"), None, "grp"),
        P(("role", "dp"), None, "grp"),
        P(("role", "dp"), "grp", None),
    )
    out_specs = P(("role", "grp", "dp"), None)
    return jax.shard_map(local, mesh=mesh, in_specs=in_specs, out_specs=out_specs, check_vma=False)
```
